128 devices in a mesh: row: 8 (over z, core), col: 16 (over x, y).
Axes of the slice: x: 4, y: 4, z: 4, core: 2. Of those that a mesh axis runs over, the one named last changes fastest.
Arguments:
- diag_inverse: float32 [1024, 1024], P(('row', 'col')), as said below
- row_basis: float32 [32, 128, 1024], P('row', 'col'), may hold values from -6 to 6
- row_coef: float32 [32, 128, 1024], P('row', 'col'), may hold values from -0.09375 to 0.09375
- row_ranks: int32 [32], P('row'), may hold values from 16 to 128, as said below
- col_basis: float32 [48, 128, 1024], P('col', 'row'), may hold values from -6 to 6
- col_coef: float32 [48, 128, 1024], P('col', 'row'), may hold values from -0.09375 to 0.09375
- col_ranks: int32 [48], P('col'), may hold values from 16 to 128, as said below
- tile_basis: float32 [32, 48, 1024, 128], P('row', 'col'), may hold values from -6 to 6
- tile_coef: float32 [32, 48, 1024, 128], P('row', 'col'), may hold values from -0.5 to 0.5
- tile_ranks: int32 [32, 48], P('row', 'col'), may hold values from 16 to 128, as said below
Outputs:
- new_basis: bfloat16 [32, 48, 1024, 128], P('row', 'col')
- new_coef: bfloat16 [32, 48, 1024, 128], P('row', 'col')
The draws below stay inside these ranges and needn't reach their ends.
Inputs may be any that keep to these rules, and one draw needn't show every extreme that they name: `row_ranks`: rank of each panel tile; the smallest and largest values occur in every draw. `col_ranks`: rank of each panel tile; the smallest and largest values occur in every draw. `tile_ranks`: rank of each trailing tile; the smallest and largest values occur in every draw. `diag_inverse`: lower triangular with a positive diagonal.
All inputs are finite; a program needn't handle non-finite values.
Results may differ from the reference program's by a relative error of at most 0.001.
Values sent between devices are 32-bit elements; how exact they have to be, the bound alone decides.
No kernel may reach another device: no remote copies, remote signals or barrier semaphores. Data moves between devices by JAX's collectives and lax.ppermute only.
A program may use at most 128 MiB of HBM per device.

```python
import math
import jax
import jax.numpy as jnp
from jax import lax

NB = 1024
RMAX = 128
RLOW = 16
NR = 32
NC = 48


def pick_ranks(key, array_shape):
    tile_count = 1
    for extent in array_shape:
        tile_count = tile_count * extent
    values = jax.random.randint(key, (tile_count,), RLOW, RMAX + 1)
    top_slot = jax.random.randint(jax.random.fold_in(key, 1), (), 0, tile_count)
    offset = jax.random.randint(jax.random.fold_in(key, 2), (), 1, tile_count)
    second = (top_slot + offset) % tile_count
    slot_ids = jnp.arange(tile_count)
    values = jnp.where(slot_ids == top_slot, RMAX, values)
    values = jnp.where(slot_ids == second, RLOW, values)
    return values.reshape(array_shape).astype(jnp.int32)


def draw_row_ranks(key, part):
    return pick_ranks(jax.random.fold_in(key, 11), (NR,))


def draw_col_ranks(key, part):
    return pick_ranks(jax.random.fold_in(key, 23), (NC,))


def draw_tile_ranks(key, part):
    return pick_ranks(jax.random.fold_in(key, 37), (NR, NC))


def draw_diag_inverse(key, part):
    seeded = jax.random.fold_in(key, 41)
    lower_part = jax.random.normal(seeded, (NB, NB), jnp.float32)
    diagonal_part = jax.random.uniform(jax.random.fold_in(key, 43), (NB,), jnp.float32, 1.0, 2.0)
    row_ids = jnp.arange(NB, dtype=jnp.int32)[:, None]
    col_ids = jnp.arange(NB, dtype=jnp.int32)[None, :]
    below = jnp.where(row_ids > col_ids, lower_part * (1.0 / NB ** 0.5), 0.0)
    return below + jnp.where(row_ids == col_ids, diagonal_part[:, None], 0.0)


def steps_of(own_key, shape, pieces, smallest, largest):
    def one(axis_at, shards_of):
        steps = jax.random.uniform(jax.random.fold_in(jax.random.fold_in(own_key, 6), axis_at), (shards_of,), jnp.float32, smallest / len(pieces), largest / len(pieces))
        return jnp.repeat(jnp.exp(steps), shape[axis_at] // shards_of).reshape((-1,) + (1,) * (len(shape) - axis_at - 1))

    loudness = one(*pieces[0])
    for cut in pieces[1:]:
        loudness = loudness * one(*cut)
    return loudness


def bell_draw(stream_key, dims, deviation, reach, cuts=(), held_as=jnp.bfloat16):
    gain = steps_of(stream_key, dims, cuts, -0.22, 0.18) if cuts else 1.0
    entries = jax.random.normal(stream_key, dims, jnp.float32) * deviation * gain
    return jnp.minimum(jnp.maximum(entries, -reach), reach).astype(held_as)


def setup_inputs(seed: int = 0) -> dict:
    key_list = jax.random.split(jax.random.key(seed), 11)
    return {
        "diag_inverse": draw_diag_inverse(jax.random.fold_in(key_list[10], 71), 0),
        "row_basis": bell_draw(key_list[1], (NR, RMAX, NB), 1.0, 6.0, ((0, 8), (1, 16)), jnp.float32),
        "row_coef": bell_draw(key_list[2], (NR, RMAX, NB), (RMAX * 32) ** -0.5, 0.09375, ((0, 8), (1, 16)), jnp.float32),
        "row_ranks": draw_row_ranks(jax.random.fold_in(key_list[10], 71), 0),
        "col_basis": bell_draw(key_list[4], (NC, RMAX, NB), 1.0, 6.0, ((0, 16), (1, 8)), jnp.float32),
        "col_coef": bell_draw(key_list[5], (NC, RMAX, NB), (RMAX * 32) ** -0.5, 0.09375, ((0, 16), (1, 8)), jnp.float32),
        "col_ranks": draw_col_ranks(jax.random.fold_in(key_list[10], 71), 0),
        "tile_basis": bell_draw(key_list[7], (NR, NC, NB, RMAX), 1.0, 6.0, ((0, 8), (1, 16)), jnp.float32),
        "tile_coef": bell_draw(key_list[8], (NR, NC, NB, RMAX), RMAX ** -0.5, 0.5, ((0, 8), (1, 16)), jnp.float32),
        "tile_ranks": draw_tile_ranks(jax.random.fold_in(key_list[10], 71), 0),
    }


HIGHEST = lax.Precision.HIGHEST

def orthonormal(sketch_block, rank_keep):
    gram_matrix = jnp.dot(sketch_block.T, sketch_block, precision=HIGHEST) + jnp.diag(1.0 - rank_keep)
    factor = jnp.linalg.cholesky(gram_matrix)
    return jax.scipy.linalg.solve_triangular(factor, sketch_block.T, lower=True).T

def recompress(tile_left, tile_right, rank_keep, left_panel, coupling, right_panel):
    tile_left = tile_left * rank_keep[None, :]
    tile_right = tile_right * rank_keep[None, :]
    inner_gram = jnp.dot(tile_right.T, tile_right, precision=HIGHEST)
    cross_term = jnp.dot(right_panel, tile_right, precision=HIGHEST)
    sketch = jnp.dot(tile_left, inner_gram, precision=HIGHEST) - jnp.dot(left_panel.T, jnp.dot(coupling, cross_term, precision=HIGHEST), precision=HIGHEST)
    ortho_basis = orthonormal(orthonormal(sketch, rank_keep), rank_keep)
    first_part = jnp.dot(tile_right, jnp.dot(tile_left.T, ortho_basis, precision=HIGHEST), precision=HIGHEST)
    left_proj = jnp.dot(left_panel, ortho_basis, precision=HIGHEST)
    second_part = jnp.dot(right_panel.T, jnp.dot(coupling.T, left_proj, precision=HIGHEST), precision=HIGHEST)
    scaled_basis = ortho_basis * math.sqrt(ortho_basis.shape[0])
    return (scaled_basis.astype(jnp.bfloat16), (first_part - second_part).astype(jnp.bfloat16))

def panel_factors(basis_rows, coef_rows, panel_ranks, inverse_factor):
    rank_keep = (jnp.arange(RMAX, dtype=jnp.int32)[None, :] < panel_ranks[:, None]).astype(jnp.float32)[:, :, None]
    basis_rows = basis_rows * rank_keep
    coef_rows = coef_rows * rank_keep
    tile_count = coef_rows.shape[0]
    flat_rows = coef_rows.reshape(tile_count * RMAX, NB)
    solved = jnp.dot(flat_rows, inverse_factor.T, precision=HIGHEST)
    return (basis_rows, solved.reshape(tile_count, RMAX, NB))

def reference(diag_inverse, row_basis, row_coef, row_ranks, col_basis, col_coef, col_ranks, tile_basis, tile_coef, tile_ranks):
    row_left, row_solved = panel_factors(row_basis, row_coef, row_ranks, diag_inverse)
    col_left, col_solved = panel_factors(col_basis, col_coef, col_ranks, diag_inverse)

    def one_tile(position):
        tile_row = position // NC
        tile_col = position % NC
        coupling = jnp.dot(row_solved[tile_row], col_solved[tile_col].T, precision=HIGHEST)
        rank_keep = (jnp.arange(RMAX, dtype=jnp.int32) < tile_ranks[tile_row, tile_col]).astype(jnp.float32)
        return recompress(tile_basis[tile_row, tile_col], tile_coef[tile_row, tile_col], rank_keep, row_left[tile_row], coupling, col_left[tile_col])
    out_basis, out_coef = lax.map(one_tile, jnp.arange(NR * NC, dtype=jnp.int32))
    return (out_basis.reshape(NR, NC, NB, RMAX), out_coef.reshape(NR, NC, NB, RMAX))
```

```python
import math

import jax
import jax.numpy as jnp
from jax import lax
from jax.experimental import pallas as pl
from jax.experimental.pallas import tpu as pltpu
from jax.sharding import PartitionSpec as P

HIGHEST = lax.Precision.HIGHEST


BF = jnp.bfloat16
F32 = jnp.float32
BLK = 32

def split3(a):
    h = a.astype(BF)
    rest = a - h.astype(F32)
    m = rest.astype(BF)
    l = (rest - m.astype(F32)).astype(BF)
    return h, m, l

def dot6(a, b, ca, cb):
    ah, am, al = split3(a)
    bh, bm, bl = split3(b)
    lhs = jnp.concatenate([ah, ah, am, ah, al, am], axis=ca)
    rhs = jnp.concatenate([bh, bm, bh, bl, bh, bm], axis=cb)
    return lax.dot_general(lhs, rhs, (((ca,), (cb,)), ((), ())), preferred_element_type=F32)

def eliminate(block, base, lanes, rows):
    groups = BLK // 8
    parts = [block[8 * g:8 * g + 8] for g in range(groups)]
    done = [jnp.zeros((8, 128), F32)] * groups
    for kk in range(BLK):
        g0, s = kk // 8, kk % 8
        k = base + kk
        at_k = lanes == k
        cols = [parts[g][:, k:k + 1] for g in range(g0, groups)]
        scale = lax.rsqrt(cols[0][s:s + 1, :])
        row = jnp.where(at_k[0:1], 1.0, parts[g0][s:s + 1, :]) * scale
        for g in range(g0, groups):
            col = cols[g - g0] * scale
            if g == g0:
                keep = jnp.where(at_k, 0.0, parts[g])
                new = keep - col * row
                parts[g] = jnp.where(rows > s, new, jnp.where(rows == s, row, parts[g]))
            else:
                parts[g] = jnp.where(at_k, 0.0, parts[g]) - col * row
    return jnp.concatenate(parts, axis=0)

def inverse_factor(work, tiles):
    lanes = lax.broadcasted_iota(jnp.int32, (8, 128), 1)
    rows = lax.broadcasted_iota(jnp.int32, (8, 128), 0)
    lane_b = lax.broadcasted_iota(jnp.int32, (BLK, 128), 1)
    row_b = lax.broadcasted_iota(jnp.int32, (BLK, 128), 0)
    for t in range(128 // BLK):
        base = t * BLK
        for m in range(tiles):
            r = eliminate(work[m, base:base + BLK, :], base, lanes, rows)
            inside = (lane_b >= base) & (lane_b < base + BLK)
            r = jnp.where(inside & (lane_b - base > row_b), 0.0, r)
            if base + BLK < 128:
                upd = dot6(r, r, 0, 0)
                rest = work[m, base + BLK:, :]
                lane_r = lax.broadcasted_iota(jnp.int32, rest.shape, 1)
                rest = jnp.where((lane_r >= base) & (lane_r < base + BLK), 0.0, rest)
                work[m, base + BLK:, :] = rest - upd[base + BLK:, :]
            work[m, base:base + BLK, :] = jnp.where(lane_b - base > row_b, 0.0, r)

def chol_kernel(g_ref, o_ref, work):
    tiles = g_ref.shape[0]
    for m in range(tiles):
        work[m] = g_ref[m]
    inverse_factor(work, tiles)
    for m in range(tiles):
        first = work[m]
        o_ref[m] = first
        second = dot6(first, dot6(g_ref[m], first, 1, 1), 1, 0)
        work[m] = 0.5 * (second + second.T)
    inverse_factor(work, tiles)
    for m in range(tiles):
        o_ref[m] = dot6(work[m], o_ref[m], 1, 0)

def chol2(g):
    return pl.pallas_call(chol_kernel, out_shape=jax.ShapeDtypeStruct(g.shape, F32),
        in_specs=[pl.BlockSpec(memory_space=pltpu.VMEM)], out_specs=pl.BlockSpec(memory_space=pltpu.VMEM),
        scratch_shapes=[pltpu.VMEM(g.shape, F32)],
        compiler_params=pltpu.CompilerParams(vmem_limit_bytes=48*2**20), name="chol2")(g)


def orthonormal_twice(sketch_block, rank_keep):
    rank_width = rank_keep.shape[-1]
    eye_one = jnp.eye(rank_width, dtype=jnp.float32)[None, :, :]
    gram_matrix = jnp.einsum("tnr,tns->trs", sketch_block, sketch_block, precision=HIGHEST)
    gram_matrix = gram_matrix + eye_one * (1.0 - rank_keep)[:, None, :]
    combined = chol2(gram_matrix)
    return jnp.einsum("tnr,tsr->tns", sketch_block, combined, precision=HIGHEST)


def share_mask(panel_ranks, rank_share, position):
    columns = position * rank_share + jnp.arange(rank_share, dtype=jnp.int32)
    return (columns[None, :] < panel_ranks[:, None]).astype(jnp.float32)[:, :, None]


def solve_rows(inverse_factor, coef_rows):
    tile_count, rank_rows, order = coef_rows.shape
    flat_rows = coef_rows.reshape(tile_count * rank_rows, order)
    solved = jnp.dot(flat_rows, inverse_factor.T, precision=HIGHEST)
    return solved.reshape(tile_count, rank_rows, order)


def body(
    diag_inverse,
    row_basis,
    row_coef,
    row_ranks,
    col_basis,
    col_coef,
    col_ranks,
    tile_basis,
    tile_coef,
    tile_ranks,
):
    inverse_whole = lax.all_gather(diag_inverse, ("row", "col"), axis=0, tiled=True)
    row_keep = share_mask(row_ranks, row_basis.shape[1], lax.axis_index("col"))
    row_left = row_basis * row_keep
    row_send = row_coef * row_keep
    row_send = solve_rows(inverse_whole, row_send)
    row_left, row_solved = (
        lax.all_gather(row_left, "col", axis=1, tiled=True),
        lax.all_gather(row_send, "col", axis=1, tiled=True),
    )
    col_keep = share_mask(col_ranks, col_basis.shape[1], lax.axis_index("row"))
    col_left = col_basis * col_keep
    col_send = col_coef * col_keep
    col_send = solve_rows(inverse_whole, col_send)
    col_left, col_solved = (
        lax.all_gather(col_left, "row", axis=1, tiled=True),
        lax.all_gather(col_send, "row", axis=1, tiled=True),
    )
    local_rows, local_cols, order, rank_width = tile_basis.shape

    def pair_product(left_rows, right_rows):
        return jnp.dot(left_rows, right_rows.T, precision=HIGHEST)

    coupling = jax.vmap(jax.vmap(pair_product, in_axes=(None, 0)), in_axes=(0, None))(
        row_solved, col_solved
    )
    tile_count = local_rows * local_cols
    rank_keep = (
        jnp.arange(rank_width, dtype=jnp.int32)[None, None, :] < tile_ranks[:, :, None]
    ).astype(jnp.float32)
    masked_left = tile_basis * rank_keep[:, :, None, :]
    masked_right = tile_coef * rank_keep[:, :, None, :]

    def make_sketch(tile_left, tile_right, left_panel, pair_coupling, right_panel):
        inner_gram = jnp.dot(tile_right.T, tile_right, precision=HIGHEST)
        cross_term = jnp.dot(right_panel, tile_right, precision=HIGHEST)
        return jnp.dot(tile_left, inner_gram, precision=HIGHEST) - jnp.dot(
            left_panel.T, jnp.dot(pair_coupling, cross_term, precision=HIGHEST), precision=HIGHEST
        )

    sketch_inner = jax.vmap(make_sketch, in_axes=(0, 0, None, 0, 0))
    sketch = jax.vmap(sketch_inner, in_axes=(0, 0, 0, 0, None))(
        masked_left, masked_right, row_left, coupling, col_left
    )
    flat_keep = rank_keep.reshape(tile_count, rank_width)
    flat_sketch = sketch.reshape(tile_count, order, rank_width)
    ortho_basis = orthonormal_twice(flat_sketch, flat_keep).reshape(
        local_rows, local_cols, order, rank_width
    )

    def make_coef(tile_left, tile_right, left_panel, pair_coupling, right_panel, basis_block):
        first_part = jnp.dot(
            tile_right, jnp.dot(tile_left.T, basis_block, precision=HIGHEST), precision=HIGHEST
        )
        left_proj = jnp.dot(left_panel, basis_block, precision=HIGHEST)
        second_part = jnp.dot(
            right_panel.T, jnp.dot(pair_coupling.T, left_proj, precision=HIGHEST), precision=HIGHEST
        )
        return first_part - second_part

    coef_inner = jax.vmap(make_coef, in_axes=(0, 0, None, 0, 0, 0))
    new_coef = jax.vmap(coef_inner, in_axes=(0, 0, 0, 0, None, 0))(
        masked_left, masked_right, row_left, coupling, col_left, ortho_basis
    )
    scaled_basis = ortho_basis * math.sqrt(order)
    return (scaled_basis.astype(jnp.bfloat16), new_coef.astype(jnp.bfloat16))


def solution(mesh):
    placed = (
        P(("row", "col"), None),
        P("row", "col", None),
        P("row", "col", None),
        P("row"),
        P("col", "row", None),
        P("col", "row", None),
        P("col"),
        P("row", "col", None, None),
        P("row", "col", None, None),
        P("row", "col"),
    )
    return jax.shard_map(
        body,
        mesh=mesh,
        in_specs=placed,
        out_specs=(P("row", "col", None, None), P("row", "col", None, None)),
        check_vma=False,
    )
```

```python
import math

import jax
import jax.numpy as jnp
from jax import lax
from jax.experimental import pallas as pl
from jax.experimental.pallas import tpu as pltpu
from jax.sharding import PartitionSpec as P

BF = jnp.bfloat16
F32 = jnp.float32
BLK = 32
TOGETHER = 4
RANK = 128
ORDER = 1024
VMEM = pltpu.VMEM


def split2(a):
    high = a.astype(BF)
    return high, (a - high.astype(F32)).astype(BF)


def dot3(a, b, ca, cb):
    ah, al = split2(a)
    bh, bl = split2(b)
    lhs = jnp.concatenate([ah, ah, al], axis=ca)
    rhs = jnp.concatenate([bh, bl, bh], axis=cb)
    return lax.dot_general(lhs, rhs, (((ca,), (cb,)), ((), ())), preferred_element_type=F32)


def dot_parts(lhs, rhs, ca, cb):
    out = lax.dot_general(lhs, rhs, (((ca,), (cb,)), ((), ())), preferred_element_type=F32)
    return (out[:RANK, :RANK] + (out[:RANK, RANK:] + out[RANK:, :RANK])) + out[RANK:, RANK:]


def wide(a, axis):
    return jnp.concatenate(split2(a), axis=axis)


def lane_mask(rank, rows):
    return lax.broadcasted_iota(jnp.int32, (rows, RANK), 1) < rank


def gram_of(a):
    both = wide(a, 1)
    out = lax.dot_general(both[:, :RANK], both, (((0,), (0,)), ((), ())), preferred_element_type=F32)
    cross = out[:, RANK:]
    return out[:, :RANK] + (cross + cross.T)


def split3(a):
    h = a.astype(BF)
    rest = a - h.astype(F32)
    m = rest.astype(BF)
    l = (rest - m.astype(F32)).astype(BF)
    return h, m, l


def dot6(a, b, ca, cb):
    ah, am, al = split3(a)
    bh, bm, bl = split3(b)
    lhs = jnp.concatenate([ah, ah, am, ah, al, am], axis=ca)
    rhs = jnp.concatenate([bh, bm, bh, bl, bh, bm], axis=cb)
    return lax.dot_general(lhs, rhs, (((ca,), (cb,)), ((), ())), preferred_element_type=F32)


def eliminate(blocks, base, lanes, rows):
    groups = BLK // 8
    parts = [[block[8 * g:8 * g + 8] for g in range(groups)] for block in blocks]
    for kk in range(BLK):
        g0, s = kk // 8, kk % 8
        k = base + kk
        at_k = lanes == k
        cols = [[p[g][:, k:k + 1] for g in range(g0, groups)] for p in parts]
        scales = [lax.rsqrt(c[0][s:s + 1, :]) for c in cols]
        lines = [jnp.where(at_k[0:1], 1.0, p[g0][s:s + 1, :]) * scale for p, scale in zip(parts, scales)]
        for p, c, scale, line in zip(parts, cols, scales, lines):
            for g in range(g0, groups):
                new = jnp.where(at_k, 0.0, p[g]) - (c[g - g0] * scale) * line
                if g == g0:
                    new = jnp.where(rows > s, new, jnp.where(rows == s, line, p[g]))
                p[g] = new
    return [jnp.concatenate(p, axis=0) for p in parts]


def inverse_factor(work, tiles):
    lanes = lax.broadcasted_iota(jnp.int32, (8, 128), 1)
    rows = lax.broadcasted_iota(jnp.int32, (8, 128), 0)
    lane_b = lax.broadcasted_iota(jnp.int32, (BLK, 128), 1)
    row_b = lax.broadcasted_iota(jnp.int32, (BLK, 128), 0)
    for t in range(128 // BLK):
        base = t * BLK
        for first in range(0, tiles, TOGETHER):
            group = range(first, first + TOGETHER)
            solved = eliminate([work[m, base:base + BLK, :] for m in group], base, lanes, rows)
            inside = (lane_b >= base) & (lane_b < base + BLK)
            for m, r in zip(group, solved):
                r = jnp.where(inside & (lane_b - base > row_b), 0.0, r)
                if base + BLK < 128:
                    upd = dot6(r, r, 0, 0)[base + BLK:, :]
                    rest = work[m, base + BLK:, :]
                    lane_r = lax.broadcasted_iota(jnp.int32, rest.shape, 1)
                    rest = jnp.where((lane_r >= base) & (lane_r < base + BLK), 0.0, rest)
                    work[m, base + BLK:, :] = rest - upd
                work[m, base:base + BLK, :] = jnp.where(lane_b - base > row_b, 0.0, r)


def inverse_twice(gram, work, comb):
    tiles = gram.shape[0]
    for m in range(tiles):
        work[m] = gram[m]
    inverse_factor(work, tiles)
    for m in range(tiles):
        first = work[m]
        comb[m] = first
        second = dot6(first, dot6(gram[m], first, 1, 1), 1, 0)
        work[m] = 0.5 * (second + second.T)
    inverse_factor(work, tiles)
    for m in range(tiles):
        comb[m] = dot6(work[m], comb[m], 1, 0)


def prep_kernel(rank_ref, p_ref, q_ref, o_ref):
    keep = lane_mask(rank_ref[pl.program_id(0)], ORDER)
    right = jnp.where(keep, q_ref[0], 0.0)
    left = jnp.where(keep, p_ref[0], 0.0)
    o_ref[0] = dot3(left, gram_of(right), 1, 0)


def prep(ranks, tile_left, tile_right):
    tiles = tile_left.shape[0]
    block = pl.BlockSpec((1, ORDER, RANK), lambda t: (t, 0, 0))
    return pl.pallas_call(
        prep_kernel,
        grid=(tiles,),
        in_specs=[pl.BlockSpec(memory_space=pltpu.SMEM), block, block],
        out_specs=block,
        out_shape=jax.ShapeDtypeStruct(tile_left.shape, F32),
        compiler_params=pltpu.CompilerParams(vmem_limit_bytes=16 * 2**20),
        cost_estimate=pl.CostEstimate(flops=tiles * 6 * 2**26, bytes_accessed=tiles * 3 * 2**19, transcendentals=0),
        name="prep",
    )(ranks, tile_left, tile_right)


def row_panel(pieces, tile, swap):
    own, left, right, low, high = pieces
    grid = []
    for first in range(4):
        for second in range(4):
            outer, inner = (second, first) if swap else (first, second)
            if outer < 3:
                grid.append((own, left, right)[outer][inner, tile])
            else:
                grid.append((low, high)[inner // 2][inner % 2, tile])
    return jnp.concatenate(grid, axis=0)


def col_panel(pieces, tile, part):
    rows = []
    for side in range(2):
        ring = pieces[5 * side:5 * side + 5]
        for ref in ring[:3]:
            rows.append(ref[3 * part + tile])
        rows.append(ring[3 + part][tile])
    return jnp.concatenate(rows, axis=0)


def couple_kernel(*refs):
    row_pieces, col_pieces = refs[:5], refs[5:15]
    factor_ref, c_ref, vh, vl, acc = refs[15:]
    rows, cols = 4, 3
    for i in range(rows + cols):
        panel = row_panel(row_pieces, i, False) if i < rows else col_panel(col_pieces, i - rows, 1)
        high, low = split2(panel)
        vh[i * RANK:(i + 1) * RANK] = high
        vl[i * RANK:(i + 1) * RANK] = low
    cut = rows * RANK
    for z in range(4):
        span = (z + 1) * (ORDER // 4)
        factor = factor_ref[z * 256:(z + 1) * 256, :span]
        dh, dl = split2(factor)
        dims = (((1,), (1,)), ((), ()))
        solved = (
            lax.dot_general(vh[:, :span], dh, dims, preferred_element_type=F32)
            + lax.dot_general(vh[:, :span], dl, dims, preferred_element_type=F32)
            + lax.dot_general(vl[:, :span], dh, dims, preferred_element_type=F32)
        )
        term = dot3(solved[:cut], solved[cut:], 1, 1)
        if z == 0:
            acc[...] = term
        else:
            acc[...] += term
    for i in range(rows):
        for j in range(cols):
            c_ref[i * cols + j] = acc[i * RANK:(i + 1) * RANK, j * RANK:(j + 1) * RANK]


def couple(row_pieces, col_pieces, factor):
    return pl.pallas_call(
        couple_kernel,
        in_specs=[pl.BlockSpec(memory_space=VMEM)] * 16,
        out_specs=pl.BlockSpec(memory_space=VMEM),
        out_shape=jax.ShapeDtypeStruct((12, RANK, RANK), F32),
        scratch_shapes=[VMEM((7 * RANK, ORDER), BF), VMEM((7 * RANK, ORDER), BF), VMEM((4 * RANK, 3 * RANK), F32)],
        compiler_params=pltpu.CompilerParams(vmem_limit_bytes=48 * 2**20),
        cost_estimate=pl.CostEstimate(flops=5 * 10**9, bytes_accessed=8 * 2**20, transcendentals=0),
        name="couple",
    )(*row_pieces, *col_pieces, factor)


def sketch_kernel(rank_ref, *refs):
    row_pieces, col_pieces = refs[:5], refs[5:15]
    c_ref, pg_ref, q_ref, x_ref, gram_ref, flat = refs[15:]
    cols = range(3)
    step = pl.program_id(0)

    @pl.when(step == 0)
    def _():
        for j in cols:
            flat[j] = wide(col_panel(col_pieces, j, 0), 0)

    ranks = [rank_ref[3 * step + j] for j in cols]
    right = [wide(jnp.where(lane_mask(ranks[j], ORDER), q_ref[j], 0.0), 1) for j in cols]
    cross = [dot_parts(flat[j], right[j], 1, 0) for j in cols]
    inner = [split2(dot3(c_ref[j], cross[j], 1, 0)) for j in cols]
    high, low = split2(row_panel(row_pieces, step, True).T)
    lhs = jnp.concatenate([high, high, low], axis=1)
    row_ids = lax.broadcasted_iota(jnp.int32, (RANK, RANK), 0)
    lane_ids = lax.broadcasted_iota(jnp.int32, (RANK, RANK), 1)
    for j in cols:
        ih, il = inner[j]
        rhs = jnp.concatenate([ih, il, ih], axis=0)
        x = pg_ref[j] - jnp.dot(lhs, rhs, preferred_element_type=F32)
        x_ref[j] = x
        gram_ref[j] = gram_of(x) + jnp.where((row_ids == lane_ids) & (row_ids >= ranks[j]), 1.0, 0.0)


def chol_kernel(gram_ref, comb_ref, work):
    inverse_twice(gram_ref, work, comb_ref)


def finish_kernel(rank_ref, *refs):
    row_pieces, col_pieces = refs[:5], refs[5:15]
    c_ref, comb_ref, x_ref, p_ref, q_ref, basis_ref, coef_ref, tall = refs[15:]
    cols = range(3)
    step = pl.program_id(0)

    @pl.when(step == 0)
    def _():
        for j in cols:
            tall[j] = wide(col_panel(col_pieces, j, 0).T, 1)

    flat = wide(row_panel(row_pieces, step, True), 0)
    for j in cols:
        keep = lane_mask(rank_ref[3 * step + j], ORDER)
        y = dot3(x_ref[j], comb_ref[j], 1, 1)
        basis_ref[j] = (y * math.sqrt(ORDER)).astype(BF)
        left = jnp.where(keep, p_ref[j], 0.0)
        right = jnp.where(keep, q_ref[j], 0.0)
        y_wide = wide(y, 1)
        from_left = dot_parts(wide(left, 1), y_wide, 0, 0)
        from_row = dot3(c_ref[j], dot_parts(flat, y_wide, 1, 0), 0, 0)
        qh, ql = split2(right)
        ah, al = split2(from_left)
        bh, bl = split2(-from_row)
        tall_j = tall[j]
        lhs = jnp.concatenate([qh, qh, ql, tall_j[:, :RANK], tall_j], axis=1)
        rhs = jnp.concatenate([ah, al, ah, bh, bl, bh], axis=0)
        coef_ref[j] = jnp.dot(lhs, rhs, preferred_element_type=F32).astype(BF)


def tiles_step(ranks, row_pieces, col_pieces, coupling, half, tile_left, tile_right):
    tiles = tile_left.shape[0]
    whole = pl.BlockSpec(memory_space=VMEM)
    scalars = pl.BlockSpec(memory_space=pltpu.SMEM)
    block = pl.BlockSpec((3, ORDER, RANK), lambda t: (t, 0, 0))
    small = pl.BlockSpec((3, RANK, RANK), lambda t: (t, 0, 0))
    params = pltpu.CompilerParams(vmem_limit_bytes=48 * 2**20)
    square = jax.ShapeDtypeStruct((tiles, RANK, RANK), F32)
    sketch, gram = pl.pallas_call(
        sketch_kernel,
        grid=(tiles // 3,),
        in_specs=[scalars] + [whole] * 15 + [small, block, block],
        out_specs=[block, small],
        out_shape=[jax.ShapeDtypeStruct(tile_left.shape, F32), square],
        scratch_shapes=[VMEM((3, 2 * RANK, ORDER), BF)],
        compiler_params=params,
        name="sketch",
    )(ranks, *row_pieces, *col_pieces, coupling, half, tile_right)
    comb = pl.pallas_call(
        chol_kernel,
        in_specs=[whole],
        out_specs=whole,
        out_shape=square,
        scratch_shapes=[VMEM((tiles, RANK, RANK), F32)],
        compiler_params=params,
        name="factors",
    )(gram)
    shape = jax.ShapeDtypeStruct(tile_left.shape, BF)
    return pl.pallas_call(
        finish_kernel,
        grid=(tiles // 3,),
        in_specs=[scalars] + [whole] * 15 + [small, small, block, block, block],
        out_specs=[block, block],
        out_shape=[shape, shape],
        scratch_shapes=[VMEM((3, ORDER, 2 * RANK), BF)],
        compiler_params=params,
        name="finish",
    )(ranks, *row_pieces, *col_pieces, coupling, comb, sketch, tile_left, tile_right)


def shift_x(v, d):
    return lax.ppermute(v, "col", [(x * 4 + y, (x + d) % 4 * 4 + y) for x in range(4) for y in range(4)])


def shift_y(v, d):
    return lax.ppermute(v, "col", [(x * 4 + y, x * 4 + (y + d) % 4) for x in range(4) for y in range(4)])


def shift_z(v, d):
    return lax.ppermute(v, "row", [(z * 2 + c, (z + d) % 4 * 2 + c) for z in range(4) for c in range(2)])


def other_core(v):
    return lax.ppermute(v, "row", [(r, r ^ 1) for r in range(8)])


def gather_small(v, shift):
    return jnp.stack([v, shift(v, 1), shift(v, -1), shift(v, 2)])


def gather_ring(v, shift):
    half = v.shape[0] // 2
    left, right = shift(v, 1), shift(v, -1)
    return [v, left, right, shift(left[:half], 1), shift(right[half:], -1)]


def share_mask(panel_ranks, rank_share, position):
    columns = position * rank_share + jnp.arange(rank_share, dtype=jnp.int32)
    return (columns[None, :] < panel_ranks[:, None]).astype(jnp.float32)[:, :, None]


def body(
    diag_inverse,
    row_basis,
    row_coef,
    row_ranks,
    col_basis,
    col_coef,
    col_ranks,
    tile_basis,
    tile_coef,
    tile_ranks,
):
    local_rows, local_cols, order, rank_width = tile_basis.shape
    tiles = local_rows * local_cols
    factor = lax.all_gather(diag_inverse, ("row", "col"), axis=0, tiled=True)

    row_keep = share_mask(row_ranks, row_basis.shape[1], lax.axis_index("col"))
    row_left = gather_ring(gather_small(row_basis * row_keep, shift_x), shift_y)
    row_right = gather_ring(gather_small(row_coef * row_keep, shift_y), shift_x)

    col_keep = share_mask(col_ranks, col_basis.shape[1], lax.axis_index("row"))
    col_both = jnp.concatenate([col_basis * col_keep, col_coef * col_keep], axis=0)
    col_ring = gather_ring(col_both, shift_z)
    col_ring = col_ring + [other_core(v) for v in col_ring]

    ranks = tile_ranks.reshape(tiles)
    left = tile_basis.reshape(tiles, order, rank_width)
    right = tile_coef.reshape(tiles, order, rank_width)
    half = prep(ranks, left, right)
    coupling = couple(row_right, col_ring, factor)
    basis, coef = tiles_step(ranks, row_left, col_ring, coupling, half, left, right)
    return (basis.reshape(tile_basis.shape), coef.reshape(tile_coef.shape))


def solution(mesh):
    placed = (
        P(("row", "col"), None),
        P("row", "col", None),
        P("row", "col", None),
        P("row"),
        P("col", "row", None),
        P("col", "row", None),
        P("col"),
        P("row", "col", None, None),
        P("row", "col", None, None),
        P("row", "col"),
    )
    return jax.shard_map(
        body,
        mesh=mesh,
        in_specs=placed,
        out_specs=(P("row", "col", None, None), P("row", "col", None, None)),
        check_vma=False,
    )
```

```python
import math

import jax
import jax.numpy as jnp
from jax import lax
from jax.experimental import pallas as pl
from jax.experimental.pallas import tpu as pltpu
from jax.sharding import PartitionSpec as P

BF = jnp.bfloat16
F32 = jnp.float32
BLK = 32
TOGETHER = 4
RANK = 128
ORDER = 1024
VMEM = pltpu.VMEM


def split2(a):
    high = a.astype(BF)
    return high, (a - high.astype(F32)).astype(BF)


def dot3(a, b, ca, cb):
    ah, al = split2(a)
    bh, bl = split2(b)
    lhs = jnp.concatenate([ah, ah, al], axis=ca)
    rhs = jnp.concatenate([bh, bl, bh], axis=cb)
    return lax.dot_general(lhs, rhs, (((ca,), (cb,)), ((), ())), preferred_element_type=F32)


def dot_parts(lhs, rhs, ca, cb):
    out = lax.dot_general(lhs, rhs, (((ca,), (cb,)), ((), ())), preferred_element_type=F32)
    return (out[:RANK, :RANK] + (out[:RANK, RANK:] + out[RANK:, :RANK])) + out[RANK:, RANK:]


def wide(a, axis):
    return jnp.concatenate(split2(a), axis=axis)


def lane_mask(rank, rows):
    return lax.broadcasted_iota(jnp.int32, (rows, RANK), 1) < rank


def gram_of(a):
    both = wide(a, 1)
    out = lax.dot_general(both[:, :RANK], both, (((0,), (0,)), ((), ())), preferred_element_type=F32)
    cross = out[:, RANK:]
    return out[:, :RANK] + (cross + cross.T)


def split3(a):
    h = a.astype(BF)
    rest = a - h.astype(F32)
    m = rest.astype(BF)
    l = (rest - m.astype(F32)).astype(BF)
    return h, m, l


def dot6(a, b, ca, cb):
    ah, am, al = split3(a)
    bh, bm, bl = split3(b)
    lhs = jnp.concatenate([ah, ah, am, ah, al, am], axis=ca)
    rhs = jnp.concatenate([bh, bm, bh, bl, bh, bm], axis=cb)
    return lax.dot_general(lhs, rhs, (((ca,), (cb,)), ((), ())), preferred_element_type=F32)


def eliminate(blocks, base, lanes, rows):
    groups = BLK // 8
    parts = [[block[8 * g:8 * g + 8] for g in range(groups)] for block in blocks]
    for kk in range(BLK):
        g0, s = kk // 8, kk % 8
        k = base + kk
        at_k = lanes == k
        cols = [[p[g][:, k:k + 1] for g in range(g0, groups)] for p in parts]
        scales = [lax.rsqrt(c[0][s:s + 1, :]) for c in cols]
        lines = [jnp.where(at_k[0:1], 1.0, p[g0][s:s + 1, :]) * scale for p, scale in zip(parts, scales)]
        for p, c, scale, line in zip(parts, cols, scales, lines):
            for g in range(g0, groups):
                new = jnp.where(at_k, 0.0, p[g]) - (c[g - g0] * scale) * line
                if g == g0:
                    new = jnp.where(rows > s, new, jnp.where(rows == s, line, p[g]))
                p[g] = new
    return [jnp.concatenate(p, axis=0) for p in parts]


def inverse_factor(work, tiles):
    lanes = lax.broadcasted_iota(jnp.int32, (8, 128), 1)
    rows = lax.broadcasted_iota(jnp.int32, (8, 128), 0)
    lane_b = lax.broadcasted_iota(jnp.int32, (BLK, 128), 1)
    row_b = lax.broadcasted_iota(jnp.int32, (BLK, 128), 0)
    for t in range(128 // BLK):
        base = t * BLK
        for first in range(0, tiles, TOGETHER):
            group = range(first, first + TOGETHER)
            solved = eliminate([work[m, base:base + BLK, :] for m in group], base, lanes, rows)
            inside = (lane_b >= base) & (lane_b < base + BLK)
            for m, r in zip(group, solved):
                r = jnp.where(inside & (lane_b - base > row_b), 0.0, r)
                if base + BLK < 128:
                    upd = dot6(r, r, 0, 0)[base + BLK:, :]
                    rest = work[m, base + BLK:, :]
                    lane_r = lax.broadcasted_iota(jnp.int32, rest.shape, 1)
                    rest = jnp.where((lane_r >= base) & (lane_r < base + BLK), 0.0, rest)
                    work[m, base + BLK:, :] = rest - upd
                work[m, base:base + BLK, :] = jnp.where(lane_b - base > row_b, 0.0, r)


def inverse_twice(gram, work, comb):
    tiles = gram.shape[0]
    for m in range(tiles):
        work[m] = gram[m]
    inverse_factor(work, tiles)
    for m in range(tiles):
        first = work[m]
        comb[m] = first
        second = dot6(first, dot6(gram[m], first, 1, 1), 1, 0)
        work[m] = 0.5 * (second + second.T)
    inverse_factor(work, tiles)
    for m in range(tiles):
        comb[m] = dot6(work[m], comb[m], 1, 0)


def prep_kernel(rank_ref, p_ref, q_ref, o_ref):
    keep = lane_mask(rank_ref[pl.program_id(0)], ORDER)
    right = jnp.where(keep, q_ref[0], 0.0)
    left = jnp.where(keep, p_ref[0], 0.0)
    o_ref[0] = dot3(left, gram_of(right), 1, 0)


def prep(ranks, tile_left, tile_right):
    tiles = tile_left.shape[0]
    block = pl.BlockSpec((1, ORDER, RANK), lambda t: (t, 0, 0))
    return pl.pallas_call(
        prep_kernel,
        grid=(tiles,),
        in_specs=[pl.BlockSpec(memory_space=pltpu.SMEM), block, block],
        out_specs=block,
        out_shape=jax.ShapeDtypeStruct(tile_left.shape, F32),
        compiler_params=pltpu.CompilerParams(vmem_limit_bytes=16 * 2**20),
        cost_estimate=pl.CostEstimate(flops=tiles * 6 * 2**26, bytes_accessed=tiles * 3 * 2**19, transcendentals=0),
        name="prep",
    )(ranks, tile_left, tile_right)


def row_panel(pieces, tile, swap):
    own, left, right, low, high = pieces
    grid = []
    for first in range(4):
        for second in range(4):
            outer, inner = (second, first) if swap else (first, second)
            if outer < 3:
                grid.append((own, left, right)[outer][inner, tile])
            else:
                grid.append((low, high)[inner // 2][inner % 2, tile])
    return jnp.concatenate(grid, axis=0)


def col_panel(pieces, tile, part):
    rows = []
    for side in range(2):
        ring = pieces[5 * side:5 * side + 5]
        for ref in ring[:3]:
            rows.append(ref[3 * part + tile])
        rows.append(ring[3 + part][tile])
    return jnp.concatenate(rows, axis=0)


def couple_kernel(*refs):
    row_pieces, col_pieces = refs[:5], refs[5:15]
    factor_ref, c_ref, vh, vl, acc = refs[15:]
    rows, cols = 4, 3
    for i in range(rows + cols):
        panel = row_panel(row_pieces, i, False) if i < rows else col_panel(col_pieces, i - rows, 1)
        high, low = split2(panel)
        vh[i * RANK:(i + 1) * RANK] = high
        vl[i * RANK:(i + 1) * RANK] = low
    cut = rows * RANK
    for z in range(4):
        span = (z + 1) * (ORDER // 4)
        factor = factor_ref[z * 256:(z + 1) * 256, :span]
        dh, dl = split2(factor)
        dims = (((1,), (1,)), ((), ()))
        solved = (
            lax.dot_general(vh[:, :span], dh, dims, preferred_element_type=F32)
            + lax.dot_general(vh[:, :span], dl, dims, preferred_element_type=F32)
            + lax.dot_general(vl[:, :span], dh, dims, preferred_element_type=F32)
        )
        term = dot3(solved[:cut], solved[cut:], 1, 1)
        if z == 0:
            acc[...] = term
        else:
            acc[...] += term
    for i in range(rows):
        for j in range(cols):
            c_ref[i * cols + j] = acc[i * RANK:(i + 1) * RANK, j * RANK:(j + 1) * RANK]


def held(arrays):
    return [pl.BlockSpec(a.shape, lambda t, n=a.ndim: (0,) * n, pipeline_mode=pl.Buffered(1)) for a in arrays]


def couple(row_pieces, col_pieces, factor):
    return pl.pallas_call(
        couple_kernel,
        grid=(1,),
        in_specs=held([*row_pieces, *col_pieces, factor]),
        out_specs=pl.BlockSpec((12, RANK, RANK), lambda t: (0, 0, 0)),
        out_shape=jax.ShapeDtypeStruct((12, RANK, RANK), F32),
        scratch_shapes=[VMEM((7 * RANK, ORDER), BF), VMEM((7 * RANK, ORDER), BF), VMEM((4 * RANK, 3 * RANK), F32)],
        compiler_params=pltpu.CompilerParams(vmem_limit_bytes=62 * 2**20),
        cost_estimate=pl.CostEstimate(flops=5 * 10**9, bytes_accessed=8 * 2**20, transcendentals=0),
        name="couple",
    )(*row_pieces, *col_pieces, factor)


def sketch_kernel(rank_ref, *refs):
    row_pieces, col_pieces = refs[:5], refs[5:15]
    c_ref, pg_ref, q_ref, x_ref, gram_ref, flat = refs[15:]
    cols = range(3)
    step = pl.program_id(0)

    @pl.when(step == 0)
    def _():
        for j in cols:
            flat[j] = wide(col_panel(col_pieces, j, 0), 0)

    ranks = [rank_ref[3 * step + j] for j in cols]
    right = [wide(jnp.where(lane_mask(ranks[j], ORDER), q_ref[j], 0.0), 1) for j in cols]
    cross = [dot_parts(flat[j], right[j], 1, 0) for j in cols]
    inner = [split2(dot3(c_ref[j], cross[j], 1, 0)) for j in cols]
    high, low = split2(row_panel(row_pieces, step, True).T)
    lhs = jnp.concatenate([high, high, low], axis=1)
    row_ids = lax.broadcasted_iota(jnp.int32, (RANK, RANK), 0)
    lane_ids = lax.broadcasted_iota(jnp.int32, (RANK, RANK), 1)
    for j in cols:
        ih, il = inner[j]
        rhs = jnp.concatenate([ih, il, ih], axis=0)
        x = pg_ref[j] - jnp.dot(lhs, rhs, preferred_element_type=F32)
        x_ref[j] = x
        gram_ref[j] = gram_of(x) + jnp.where((row_ids == lane_ids) & (row_ids >= ranks[j]), 1.0, 0.0)


def chol_kernel(gram_ref, comb_ref, work):
    inverse_twice(gram_ref, work, comb_ref)


def finish_kernel(rank_ref, *refs):
    row_pieces, col_pieces = refs[:5], refs[5:15]
    c_ref, comb_ref, x_ref, p_ref, q_ref, basis_ref, coef_ref, tall = refs[15:]
    cols = range(3)
    step = pl.program_id(0)

    @pl.when(step == 0)
    def _():
        for j in cols:
            tall[j] = wide(col_panel(col_pieces, j, 0).T, 1)

    flat = wide(row_panel(row_pieces, step, True), 0)
    for j in cols:
        keep = lane_mask(rank_ref[3 * step + j], ORDER)
        y = dot3(x_ref[j], comb_ref[j], 1, 1)
        basis_ref[j] = (y * math.sqrt(ORDER)).astype(BF)
        left = jnp.where(keep, p_ref[j], 0.0)
        right = jnp.where(keep, q_ref[j], 0.0)
        y_wide = wide(y, 1)
        from_left = dot_parts(wide(left, 1), y_wide, 0, 0)
        from_row = dot3(c_ref[j], dot_parts(flat, y_wide, 1, 0), 0, 0)
        qh, ql = split2(right)
        ah, al = split2(from_left)
        bh, bl = split2(-from_row)
        tall_j = tall[j]
        lhs = jnp.concatenate([qh, qh, ql, tall_j[:, :RANK], tall_j], axis=1)
        rhs = jnp.concatenate([ah, al, ah, bh, bl, bh], axis=0)
        coef_ref[j] = jnp.dot(lhs, rhs, preferred_element_type=F32).astype(BF)


def tiles_step(ranks, row_pieces, col_pieces, coupling, half, tile_left, tile_right):
    tiles = tile_left.shape[0]
    whole = pl.BlockSpec(memory_space=VMEM)
    scalars = pl.BlockSpec(memory_space=pltpu.SMEM)
    block = pl.BlockSpec((3, ORDER, RANK), lambda t: (t, 0, 0))
    small = pl.BlockSpec((3, RANK, RANK), lambda t: (t, 0, 0))
    pieces = held([*row_pieces, *col_pieces])
    params = pltpu.CompilerParams(vmem_limit_bytes=62 * 2**20)
    square = jax.ShapeDtypeStruct((tiles, RANK, RANK), F32)
    sketch, gram = pl.pallas_call(
        sketch_kernel,
        grid=(tiles // 3,),
        in_specs=[scalars] + pieces + [small, block, block],
        out_specs=[block, small],
        out_shape=[jax.ShapeDtypeStruct(tile_left.shape, F32), square],
        scratch_shapes=[VMEM((3, 2 * RANK, ORDER), BF)],
        compiler_params=params,
        name="sketch",
    )(ranks, *row_pieces, *col_pieces, coupling, half, tile_right)
    comb = pl.pallas_call(
        chol_kernel,
        in_specs=[whole],
        out_specs=whole,
        out_shape=square,
        scratch_shapes=[VMEM((tiles, RANK, RANK), F32)],
        compiler_params=params,
        name="factors",
    )(gram)
    shape = jax.ShapeDtypeStruct(tile_left.shape, BF)
    return pl.pallas_call(
        finish_kernel,
        grid=(tiles // 3,),
        in_specs=[scalars] + pieces + [small, small, block, block, block],
        out_specs=[block, block],
        out_shape=[shape, shape],
        scratch_shapes=[VMEM((3, ORDER, 2 * RANK), BF)],
        compiler_params=params,
        name="finish",
    )(ranks, *row_pieces, *col_pieces, coupling, comb, sketch, tile_left, tile_right)


def shift_x(v, d):
    return lax.ppermute(v, "col", [(x * 4 + y, (x + d) % 4 * 4 + y) for x in range(4) for y in range(4)])


def shift_y(v, d):
    return lax.ppermute(v, "col", [(x * 4 + y, x * 4 + (y + d) % 4) for x in range(4) for y in range(4)])


def shift_z(v, d):
    return lax.ppermute(v, "row", [(z * 2 + c, (z + d) % 4 * 2 + c) for z in range(4) for c in range(2)])


def other_core(v):
    return lax.ppermute(v, "row", [(r, r ^ 1) for r in range(8)])


def gather_small(v, shift):
    return jnp.stack([v, shift(v, 1), shift(v, -1), shift(v, 2)])


def gather_ring(v, shift):
    half = v.shape[0] // 2
    left, right = shift(v, 1), shift(v, -1)
    return [v, left, right, shift(left[:half], 1), shift(right[half:], -1)]


def share_mask(panel_ranks, rank_share, position):
    columns = position * rank_share + jnp.arange(rank_share, dtype=jnp.int32)
    return (columns[None, :] < panel_ranks[:, None]).astype(jnp.float32)[:, :, None]


def body(
    diag_inverse,
    row_basis,
    row_coef,
    row_ranks,
    col_basis,
    col_coef,
    col_ranks,
    tile_basis,
    tile_coef,
    tile_ranks,
):
    local_rows, local_cols, order, rank_width = tile_basis.shape
    tiles = local_rows * local_cols
    factor = lax.all_gather(diag_inverse, ("row", "col"), axis=0, tiled=True)

    row_keep = share_mask(row_ranks, row_basis.shape[1], lax.axis_index("col"))
    row_left = gather_ring(gather_small(row_basis * row_keep, shift_x), shift_y)
    row_right = gather_ring(gather_small(row_coef * row_keep, shift_y), shift_x)

    col_keep = share_mask(col_ranks, col_basis.shape[1], lax.axis_index("row"))
    col_both = jnp.concatenate([col_basis * col_keep, col_coef * col_keep], axis=0)
    col_ring = gather_ring(col_both, shift_z)
    col_ring = col_ring + [other_core(v) for v in col_ring]

    ranks = tile_ranks.reshape(tiles)
    left = tile_basis.reshape(tiles, order, rank_width)
    right = tile_coef.reshape(tiles, order, rank_width)
    half = prep(ranks, left, right)
    coupling = couple(row_right, col_ring, factor)
    basis, coef = tiles_step(ranks, row_left, col_ring, coupling, half, left, right)
    return (basis.reshape(tile_basis.shape), coef.reshape(tile_coef.shape))


def solution(mesh):
    placed = (
        P(("row", "col"), None),
        P("row", "col", None),
        P("row", "col", None),
        P("row"),
        P("col", "row", None),
        P("col", "row", None),
        P("col"),
        P("row", "col", None, None),
        P("row", "col", None, None),
        P("row", "col"),
    )
    return jax.shard_map(
        body,
        mesh=mesh,
        in_specs=placed,
        out_specs=(P("row", "col", None, None), P("row", "col", None, None)),
        check_vma=False,
    )
```
